512 devices in a mesh: outer: 64 (over z_lo, y, x), inner: 8 (over z_hi, core).
Axes of the slice: x: 4, y: 4, z: 16 (z_hi: 4, z_lo: 4; z = z_hi * 4 + z_lo), core: 2. Of those that a mesh axis runs over, the one named last changes fastest.
Arguments:
- queries: bfloat16 [65536, 2048], P(('outer', 'inner')), may hold values from -6 to 6
- keys: bfloat16 [65536, 2048], P(('outer', 'inner')), may hold values from -6 to 6
- values: bfloat16 [65536, 2048], P(('outer', 'inner')), may hold values from -6 to 6
- grad_out: bfloat16 [65536, 2048], P(('outer', 'inner')), may hold values from -48 to 48
- lse: bfloat16 [65536, 16], P(('outer', 'inner')), may hold values from 4 to 7
- delta: bfloat16 [65536, 16], P(('outer', 'inner')), may hold values from -360 to 360
- span_table: int32 [512, 2], replicated, may hold values from 0 to 1023, as said below
Outputs:
- grad_queries: float32 [65536, 2048], P(('outer', 'inner'))
- grad_keys: float32 [65536, 2048], P(('outer', 'inner'))
- grad_values: float32 [65536, 2048], P(('outer', 'inner'))
The draws below stay inside these ranges and needn't reach their ends.
Inputs may be any that keep to these rules, and one draw needn't show every extreme that they name: `span_table`: row d is (c, 1023 - c); the first column is a permutation of 0 to 511.
All inputs are finite; a program needn't handle non-finite values.
Results may differ from the reference program's by a relative error of at most 0.014.
Values may be sent and summed in bfloat16 or wider, within the bound.
No kernel may reach another device: no remote copies, remote signals or barrier semaphores. Data moves between devices by JAX's collectives and lax.ppermute only.
A program may use at most 64 MiB of HBM per device.

```python
import jax
import jax.numpy as jnp
from jax import lax

HEADS = 16
HD = 128
TOK_DEV = 128
TOKENS = 65536
N_OUTER = 64
N_INNER = 8
DEVICES = 512


def draw_span_table(key, part):
    key = jax.random.fold_in(key, 11)
    order = jax.random.permutation(key, DEVICES).astype(jnp.int32)
    return jnp.stack([order, 2 * DEVICES - 1 - order], axis=1).astype(jnp.int32)


def block_levels(own_key, extent, split, low, largest):
    factor_of, own = 1.0, jax.random.fold_in(own_key, 6)
    for position, blocks in split:
        draws = jnp.exp(jax.random.uniform(jax.random.fold_in(own, position), (blocks,), jnp.float32, low / len(split), largest / len(split)))
        factor_of = factor_of * jnp.repeat(draws, extent[position] // blocks).reshape([-1 if axis == position else 1 for axis in range(len(extent))])
    return factor_of


def scatter_about(rng, shape, deviation, reach, shards=(), held_as=jnp.bfloat16):
    array = deviation * jax.random.normal(rng, shape, jnp.float32)
    if shards:
        array = array * block_levels(rng, shape, shards, -0.22, 0.18)
    return jnp.clip(array, -reach, reach).astype(held_as)


def setup_inputs(seed: int = 0) -> dict:
    key_of = jax.random.split(jax.random.key(seed), 8)
    return {
        "queries": scatter_about(key_of[0], (TOKENS, HEADS * HD), 1.0, 6.0, ((0, 512),)),
        "keys": scatter_about(key_of[1], (TOKENS, HEADS * HD), 1.0, 6.0, ((0, 512),)),
        "values": scatter_about(key_of[2], (TOKENS, HEADS * HD), 1.0, 6.0, ((0, 512),)),
        "grad_out": scatter_about(key_of[3], (TOKENS, HEADS * HD), 8.0, 48.0, ((0, 512),)),
        "lse": jnp.clip(4.0 + 3.0 * jax.random.uniform(key_of[4], (TOKENS, HEADS), jnp.float32) ** block_levels(key_of[4], (TOKENS, HEADS), ((0, 512),), -0.2, 0.2), 4.0, 7.0).astype(jnp.bfloat16),
        "delta": scatter_about(key_of[5], (TOKENS, HEADS), 60.0, 360.0, ((0, 512),)),
        "span_table": draw_span_table(jax.random.fold_in(key_of[7], 71), 0),
    }


def token_positions(table):
    half = TOK_DEV // 2
    flat = table.reshape(-1)
    return (jnp.repeat(flat, half) * half + jnp.tile(jnp.arange(half, dtype=jnp.int32), flat.shape[0])).astype(jnp.int32)


def pair_grads(qrows, dorows, lserows, deltarows, qpos, krows, vrows, kpos):
    scale = HD ** -0.5
    hp = lax.Precision.HIGHEST
    q3 = qrows.reshape(qrows.shape[0], HEADS, HD).astype(jnp.float32)
    o3 = dorows.reshape(dorows.shape[0], HEADS, HD).astype(jnp.float32)
    k3 = krows.reshape(krows.shape[0], HEADS, HD).astype(jnp.float32)
    v3 = vrows.reshape(vrows.shape[0], HEADS, HD).astype(jnp.float32)
    scores = jnp.einsum("qhd,khd->hqk", q3, k3, precision=hp)
    allowed = kpos[None, :] <= qpos[:, None]
    lse_t = lserows.astype(jnp.float32).T
    delta_t = deltarows.astype(jnp.float32).T
    probs = jnp.where(allowed[None], jnp.exp(scores * scale - lse_t[:, :, None]), 0.0)
    probs16 = probs.astype(jnp.bfloat16).astype(jnp.float32)
    grad_v = jnp.einsum("hqk,qhd->khd", probs16, o3, precision=hp)
    dprob = jnp.einsum("qhd,khd->hqk", o3, v3, precision=hp)
    dscore = (probs * (dprob - delta_t[:, :, None])).astype(jnp.bfloat16).astype(jnp.float32)
    part_q = (scale * jnp.einsum("hqk,khd->qhd", dscore, k3, precision=hp)).astype(jnp.bfloat16)
    grad_k = scale * jnp.einsum("hqk,qhd->khd", dscore, q3, precision=hp)
    width = HEADS * HD
    return part_q.reshape(-1, width), grad_k.reshape(-1, width), grad_v.reshape(-1, width)


def reference(queries, keys, values, grad_out, lse, delta, span_table):
    group_rows = N_INNER * TOK_DEV
    width = HEADS * HD
    pos = token_positions(span_table).reshape(N_OUTER, group_rows)
    qg = queries.reshape(N_OUTER, group_rows, width)
    og = grad_out.reshape(N_OUTER, group_rows, width)
    kg = keys.reshape(N_OUTER, group_rows, width)
    vg = values.reshape(N_OUTER, group_rows, width)
    lg = lse.reshape(N_OUTER, group_rows, HEADS)
    dg = delta.reshape(N_OUTER, group_rows, HEADS)

    def one_group(group):
        source = (group + N_OUTER - 1) % N_OUTER
        qpos = pos[group]
        kall = kg[source]
        vall = vg[source]
        kpos_all = pos[source]
        total_q = jnp.zeros((group_rows, width), jnp.float32)
        kparts = []
        vparts = []
        for inner_idx in range(N_INNER):
            lo = inner_idx * TOK_DEV
            part_q, grad_k, grad_v = pair_grads(qg[group], og[group], lg[group], dg[group], qpos,
                                                kall[lo:lo + TOK_DEV], vall[lo:lo + TOK_DEV], kpos_all[lo:lo + TOK_DEV])
            total_q = total_q + part_q.astype(jnp.float32)
            kparts.append(grad_k)
            vparts.append(grad_v)
        return total_q, jnp.concatenate(kparts, 0), jnp.concatenate(vparts, 0)

    grad_q, grad_k, grad_v = lax.map(one_group, jnp.arange(N_OUTER, dtype=jnp.int32))
    grad_k = jnp.roll(grad_k, -1, axis=0)
    grad_v = jnp.roll(grad_v, -1, axis=0)
    return (grad_q.reshape(TOKENS, width), grad_k.reshape(TOKENS, width), grad_v.reshape(TOKENS, width))
```

```python
import jax
import jax.numpy as jnp
from jax import lax
from jax.experimental import pallas as pl
from jax.experimental.pallas import tpu as pltpu
from jax.sharding import PartitionSpec as P

N_INNER = 8
WIDTH = 128
PAIR = 2 * WIDTH
STAT_ROWS = 16
LOG2E = 1.4426950408889634
SHIFTS = ((2, 0), (2, 1), (1, 0), (1, 1), (3, 0), (3, 1), (0, 1), (0, 0))


def moved_inner(i, shift, sign=1):
    dz, dc = shift
    return ((i // 2 + sign * dz) % 4) * 2 + (i + dc) % 2


def send_pairs(outer_count, shift, back):
    pairs = []
    for o in range(outer_count):
        for i in range(N_INNER):
            here = o * N_INNER + i
            there = ((o - 1) % outer_count) * N_INNER + moved_inner(i, shift)
            pairs.append((there, here) if back else (here, there))
    return pairs


def pack_kv(keys, values):
    rows = keys.shape[0]

    def kernel(k_ref, v_ref, out_ref, sem):
        copies = []
        for j in range(N_INNER):
            cols = pl.ds(j * PAIR, PAIR)
            copies.append(pltpu.make_async_copy(k_ref.at[:, cols], out_ref.at[j, pl.ds(0, rows)], sem.at[0, j]))
            copies.append(pltpu.make_async_copy(v_ref.at[:, cols], out_ref.at[j, pl.ds(rows, rows)], sem.at[1, j]))
        for c in copies:
            c.start()
        for c in copies:
            c.wait()

    return pl.pallas_call(
        kernel,
        out_shape=jax.ShapeDtypeStruct((N_INNER, 2 * rows, PAIR), keys.dtype),
        in_specs=[pl.BlockSpec(memory_space=pl.ANY)] * 2,
        out_specs=pl.BlockSpec(memory_space=pl.ANY),
        scratch_shapes=[pltpu.SemaphoreType.DMA((2, N_INNER))],
        name="pack_kv",
    )(keys, values)


def pack_q(chunk, queries, grad_out, stats):
    rows = queries.shape[0]

    def kernel(chunk_ref, q_ref, o_ref, s_ref, *rest):
        outs, sem = rest[:-1], rest[-1]
        copies = []
        for r, out in enumerate(outs):
            j = chunk_ref[r]
            cols = pl.ds(pl.multiple_of(j * PAIR, PAIR), PAIR)
            copies.append(pltpu.make_async_copy(q_ref.at[:, cols], out.at[pl.ds(0, rows)], sem.at[0, r]))
            copies.append(pltpu.make_async_copy(o_ref.at[:, cols], out.at[pl.ds(rows, rows)], sem.at[1, r]))
            copies.append(pltpu.make_async_copy(s_ref.at[j], out.at[pl.ds(2 * rows, STAT_ROWS)], sem.at[2, r]))
        for c in copies:
            c.start()
        for c in copies:
            c.wait()

    return pl.pallas_call(
        kernel,
        out_shape=[jax.ShapeDtypeStruct((2 * rows + STAT_ROWS, PAIR), queries.dtype)] * N_INNER,
        in_specs=[pl.BlockSpec(memory_space=pltpu.SMEM)] + [pl.BlockSpec(memory_space=pl.ANY)] * 3,
        out_specs=[pl.BlockSpec(memory_space=pl.ANY)] * N_INNER,
        scratch_shapes=[pltpu.SemaphoreType.DMA((3, N_INNER))],
        name="pack_q",
    )(chunk, queries, grad_out, stats)


def attend(kv, parts, kcol, qrow):
    rows = kv.shape[1] // 2
    half = rows // 2
    side = N_INNER * half
    scale = WIDTH ** -0.5
    tile = 256

    def kernel(kv_ref, kcol_ref, qrow_ref, *rest):
        ins, rest = rest[:N_INNER], rest[N_INNER:]
        dqs, rest = rest[:N_INNER], rest[N_INNER:]
        dkv_ref, q_s, o_s, k_s, v_s, l_s, d_s, dk_s, dv_s = rest
        for a in range(N_INNER):
            for part in range(2):
                to = pl.ds(part * side + a * half, half)
                at = part * half
                q_s[to, :] = ins[a][pl.ds(at, half), :]
                o_s[to, :] = ins[a][pl.ds(rows + at, half), :]
                k_s[to, :] = kv_ref[a, pl.ds(at, half), :]
                v_s[to, :] = kv_ref[a, pl.ds(rows + at, half), :]
            st = ins[a][pl.ds(2 * rows, STAT_ROWS), :].astype(jnp.float32)
            for h in range(2):
                for part in range(2):
                    lanes = slice(h * WIDTH + part * half, h * WIDTH + (part + 1) * half)
                    to = pl.ds(part * side + a * half, half)
                    l_s[pl.ds(h, 1), to] = st[0:1, lanes] * LOG2E
                    d_s[pl.ds(h, 1), to] = st[1:2, lanes]
        nt = (((1,), (1,)), ((), ()))
        f32 = jnp.float32
        for h in range(2):
            head = pl.ds(h * WIDTH, WIDTH)
            k_all = k_s[:, head]
            v_all = v_s[:, head]
            kt = k_all.astype(f32).T.astype(jnp.bfloat16)
            for step, (part, piece) in enumerate(((1, 0), (1, 1), (0, 0), (0, 1))):
                qs = pl.ds(part * side + piece * tile, tile)
                q = q_s[qs, head]
                o = o_s[qs, head]
                count = 2 * side if part else side
                l = l_s[pl.ds(h, 1), qs]
                d = d_s[pl.ds(h, 1), qs]
                s = lax.dot_general(k_all[:count], q, nt, preferred_element_type=f32)
                p = jnp.exp2(s * (scale * LOG2E) - l)
                qc = qrow_ref[:, pl.ds(piece * tile, tile)]
                if part:
                    p = jnp.concatenate([p[:side], jnp.where(kcol_ref[...] > qc, p[side:], 0.0)], 0)
                else:
                    p = jnp.where(kcol_ref[...] < qc, p, 0.0)
                dp = lax.dot_general(v_all[:count], o, nt, preferred_element_type=f32)
                ds = (p * (dp - d)).astype(jnp.bfloat16)
                dv = jnp.dot(p.astype(jnp.bfloat16), o, preferred_element_type=f32)
                dk = jnp.dot(ds, q, preferred_element_type=f32)
                dqt = jnp.dot(kt[:, :count], ds, preferred_element_type=f32)
                dq = (dqt * scale).T.astype(jnp.bfloat16)
                per = tile // half
                for a in range(per):
                    dqs[piece * per + a][pl.ds(part * half, half), head] = dq[a * half:(a + 1) * half]
                if step == 0:
                    dv_s[...] = dv
                    dk_s[...] = dk
                else:
                    dv_s[pl.ds(0, count), :] += dv
                    dk_s[pl.ds(0, count), :] += dk
            for b in range(N_INNER):
                for part in range(2):
                    at = pl.ds(part * side + b * half, half)
                    dkv_ref[b, pl.ds(part * half, half), head] = (dk_s[at, :] * scale).astype(jnp.bfloat16)
                    dkv_ref[b, pl.ds(rows + part * half, half), head] = dv_s[at, :].astype(jnp.bfloat16)

    vmem = pl.BlockSpec(memory_space=pltpu.VMEM)
    outs = pl.pallas_call(
        kernel,
        out_shape=[jax.ShapeDtypeStruct((rows, PAIR), jnp.bfloat16)] * N_INNER
        + [jax.ShapeDtypeStruct(kv.shape, jnp.bfloat16)],
        in_specs=[vmem] * (3 + N_INNER),
        out_specs=[vmem] * (N_INNER + 1),
        scratch_shapes=[pltpu.VMEM((2 * side, PAIR), jnp.bfloat16)] * 4
        + [pltpu.VMEM((2, 2 * side), jnp.float32)] * 2
        + [pltpu.VMEM((2 * side, WIDTH), jnp.float32)] * 2,
        compiler_params=pltpu.CompilerParams(vmem_limit_bytes=40 * 1024 * 1024),
        name="attend",
    )(kv, kcol, qrow, *parts)
    return outs[:N_INNER], outs[N_INNER]


def unpack_q(chunk, parts):
    rows = parts[0].shape[0]

    def kernel(chunk_ref, *rest):
        out = rest[-1]
        for r in range(N_INNER):
            cols = pl.ds(pl.multiple_of(chunk_ref[r] * PAIR, PAIR), PAIR)
            out[:, cols] = rest[r][...].astype(jnp.float32)

    vmem = pl.BlockSpec(memory_space=pltpu.VMEM)
    return pl.pallas_call(
        kernel,
        out_shape=jax.ShapeDtypeStruct((rows, N_INNER * PAIR), jnp.float32),
        in_specs=[pl.BlockSpec(memory_space=pltpu.SMEM)] + [vmem] * N_INNER,
        out_specs=vmem,
        name="unpack_q",
    )(chunk, *parts)


def unpack_kv(dkv):
    rows = dkv.shape[1] // 2

    def kernel(in_ref, dk_ref, dv_ref):
        dk_ref[...] = in_ref[0, pl.ds(0, rows), :].astype(jnp.float32)
        dv_ref[...] = in_ref[0, pl.ds(rows, rows), :].astype(jnp.float32)

    return pl.pallas_call(
        kernel,
        grid=(N_INNER,),
        out_shape=[jax.ShapeDtypeStruct((rows, N_INNER * PAIR), jnp.float32)] * 2,
        in_specs=[pl.BlockSpec((1, 2 * rows, PAIR), lambda j: (j, 0, 0))],
        out_specs=[pl.BlockSpec((rows, PAIR), lambda j: (0, j))] * 2,
        name="unpack_kv",
    )(dkv)


def shards(queries, keys, values, grad_out, lse, delta, span_table):
    outer_count = lax.axis_size("outer")
    outer_idx = lax.axis_index("outer")
    inner_idx = lax.axis_index("inner")
    rows = queries.shape[0]
    half = rows // 2
    chunk = jnp.stack([moved_inner(inner_idx, s) for s in SHIFTS]).astype(jnp.int32)
    senders = jnp.stack([moved_inner(inner_idx, s, -1) for s in SHIFTS]).astype(jnp.int32)

    kv = lax.all_to_all(pack_kv(keys, values), "inner", 0, 0, tiled=True)

    stats = jnp.stack([lse.T.reshape(N_INNER, PAIR), delta.T.reshape(N_INNER, PAIR)], axis=1)
    stats = jnp.pad(stats, ((0, 0), (0, STAT_ROWS - 2), (0, 0)))
    sent = pack_q(chunk, queries, grad_out, stats)
    axes = ("outer", "inner")
    parts = [lax.ppermute(x, axes, send_pairs(outer_count, s, False)) for x, s in zip(sent, SHIFTS)]

    first = span_table[:, 0].reshape(outer_count, N_INNER)
    key_c = lax.dynamic_index_in_dim(first, outer_idx, 0, keepdims=False)
    query_c = lax.dynamic_index_in_dim(first, (outer_idx + 1) % outer_count, 0, keepdims=False)[senders]
    kcol = jnp.repeat(key_c, half)[:, None]
    qrow = jnp.repeat(query_c, half)[None, :]

    dqs, dkv = attend(kv, parts, kcol, qrow)
    dkv = lax.all_to_all(dkv, "inner", 0, 0, tiled=True)
    back = [lax.ppermute(x, axes, send_pairs(outer_count, s, True)) for x, s in zip(dqs, SHIFTS)]
    grad_k, grad_v = unpack_kv(dkv)
    grad_q = unpack_q(chunk, back)
    return grad_q, grad_k, grad_v


def solution(mesh):
    placed = P(("outer", "inner"), None)
    return jax.shard_map(
        shards,
        mesh=mesh,
        in_specs=(placed,) * 6 + (P(),),
        out_specs=(placed,) * 3,
        check_vma=False,
    )
```

```python
import jax
import jax.numpy as jnp
from jax import lax
from jax.experimental import pallas as pl
from jax.experimental.pallas import tpu as pltpu
from jax.sharding import PartitionSpec as P

N_INNER = 8
WIDTH = 128
PAIR = 2 * WIDTH
STAT_ROWS = 16
LOG2E = 1.4426950408889634
CHIPS = 4


def moved_inner(i, dz, dc, sign=1):
    return ((i // 2 + sign * dz) % 4) * 2 + (i + dc) % 2


def send_pairs(outer_count, dz, back):
    pairs = []
    for o in range(outer_count):
        for i in range(N_INNER):
            here = o * N_INNER + i
            there = ((o - 1) % outer_count) * N_INNER + moved_inner(i, dz, 0)
            pairs.append((there, here) if back else (here, there))
    return pairs


def to_sibling(x):
    return lax.ppermute(x, "inner", [(i, i ^ 1) for i in range(N_INNER)])


VMEM = pl.BlockSpec(memory_space=pltpu.VMEM)
SMEM = pl.BlockSpec(memory_space=pltpu.SMEM)


def pack_kv(keys, values):
    rows = keys.shape[0]

    def kernel(k_ref, v_ref, out_ref):
        for j in range(N_INNER):
            cols = pl.ds(j * PAIR, PAIR)
            out_ref[j, pl.ds(0, rows), :] = k_ref[:, cols]
            out_ref[j, pl.ds(rows, rows), :] = v_ref[:, cols]

    return pl.pallas_call(
        kernel,
        out_shape=jax.ShapeDtypeStruct((N_INNER, 2 * rows, PAIR), keys.dtype),
        in_specs=[VMEM] * 2,
        out_specs=VMEM,
        name="pack_kv",
    )(keys, values)


def chunk_of(q_ref, o_ref, s_ref, j, out, at):
    rows = q_ref.shape[0]
    cols = pl.ds(pl.multiple_of(j * PAIR, PAIR), PAIR)
    out[at + (pl.ds(0, rows), slice(None))] = q_ref[:, cols]
    out[at + (pl.ds(rows, rows), slice(None))] = o_ref[:, cols]
    out[at + (pl.ds(2 * rows, STAT_ROWS), slice(None))] = s_ref[j]


def pack_for_sibling(chunk, queries, grad_out, stats):
    rows = queries.shape[0]

    def kernel(chunk_ref, q_ref, o_ref, s_ref, out_ref):
        for dz in range(CHIPS):
            chunk_of(q_ref, o_ref, s_ref, chunk_ref[2 * dz + 1], out_ref, (dz,))

    return pl.pallas_call(
        kernel,
        out_shape=jax.ShapeDtypeStruct((CHIPS, 2 * rows + STAT_ROWS, PAIR), queries.dtype),
        in_specs=[SMEM] + [VMEM] * 3,
        out_specs=VMEM,
        name="pack_for_sibling",
    )(chunk, queries, grad_out, stats)


def pack_q(chunk, queries, grad_out, stats, from_sibling):
    rows = queries.shape[0]

    def kernel(chunk_ref, q_ref, o_ref, s_ref, x_ref, *outs):
        for dz, out in enumerate(outs):
            chunk_of(q_ref, o_ref, s_ref, chunk_ref[2 * dz], out, (0,))
            out[1] = x_ref[dz]

    return pl.pallas_call(
        kernel,
        out_shape=[jax.ShapeDtypeStruct((2, 2 * rows + STAT_ROWS, PAIR), queries.dtype)] * CHIPS,
        in_specs=[SMEM] + [VMEM] * 4,
        out_specs=[VMEM] * CHIPS,
        name="pack_q",
    )(chunk, queries, grad_out, stats, from_sibling)


def pack_dq(own, from_sibling):
    def kernel(own_ref, x_ref, *outs):
        for dz, out in enumerate(outs):
            out[0] = own_ref[dz]
            out[1] = x_ref[dz]

    return pl.pallas_call(
        kernel,
        out_shape=[jax.ShapeDtypeStruct((2,) + own.shape[1:], own.dtype)] * CHIPS,
        in_specs=[VMEM] * 2,
        out_specs=[VMEM] * CHIPS,
        name="pack_dq",
    )(own, from_sibling)


def attend(kv, parts, kcol, qrow):
    rows = kv.shape[1] // 2
    half = rows // 2
    side = N_INNER * half
    scale = WIDTH ** -0.5
    tile = 256

    def kernel(kv_ref, kcol_ref, qrow_ref, *rest):
        ins, rest = rest[:CHIPS], rest[CHIPS:]
        ins = [ins[a // 2].at[a % 2] for a in range(N_INNER)]
        dqs = [rest[a % 2].at[a // 2] for a in range(N_INNER)]
        dkv_ref, q_s, o_s, k_s, v_s, l_s, d_s, dk_s, dv_s = rest[2:]
        for a in range(N_INNER):
            for part in range(2):
                to = pl.ds(part * side + a * half, half)
                at = part * half
                q_s[to, :] = ins[a][pl.ds(at, half), :]
                o_s[to, :] = ins[a][pl.ds(rows + at, half), :]
                k_s[to, :] = kv_ref[a, pl.ds(at, half), :]
                v_s[to, :] = kv_ref[a, pl.ds(rows + at, half), :]
            st = ins[a][pl.ds(2 * rows, STAT_ROWS), :].astype(jnp.float32)
            for h in range(2):
                for part in range(2):
                    lanes = slice(h * WIDTH + part * half, h * WIDTH + (part + 1) * half)
                    to = pl.ds(part * side + a * half, half)
                    l_s[pl.ds(h, 1), to] = st[0:1, lanes] * LOG2E
                    d_s[pl.ds(h, 1), to] = st[1:2, lanes]
        nt = (((1,), (1,)), ((), ()))
        f32 = jnp.float32
        for h in range(2):
            head = pl.ds(h * WIDTH, WIDTH)
            k_all = k_s[:, head]
            v_all = v_s[:, head]
            kt = k_all.astype(f32).T.astype(jnp.bfloat16)
            for step, (part, piece) in enumerate(((1, 0), (1, 1), (0, 0), (0, 1))):
                qs = pl.ds(part * side + piece * tile, tile)
                q = q_s[qs, head]
                o = o_s[qs, head]
                count = 2 * side if part else side
                l = l_s[pl.ds(h, 1), qs]
                d = d_s[pl.ds(h, 1), qs]
                s = lax.dot_general(k_all[:count], q, nt, preferred_element_type=f32)
                p = jnp.exp2(s * (scale * LOG2E) - l)
                qc = qrow_ref[:, pl.ds(piece * tile, tile)]
                if part:
                    p = jnp.concatenate([p[:side], jnp.where(kcol_ref[...] > qc, p[side:], 0.0)], 0)
                else:
                    p = jnp.where(kcol_ref[...] < qc, p, 0.0)
                dp = lax.dot_general(v_all[:count], o, nt, preferred_element_type=f32)
                ds = (p * (dp - d)).astype(jnp.bfloat16)
                dv = jnp.dot(p.astype(jnp.bfloat16), o, preferred_element_type=f32)
                dk = jnp.dot(ds, q, preferred_element_type=f32)
                dqt = jnp.dot(kt[:, :count], ds, preferred_element_type=f32)
                dq = (dqt * scale).T.astype(jnp.bfloat16)
                per = tile // half
                for a in range(per):
                    dqs[piece * per + a][pl.ds(part * half, half), head] = dq[a * half:(a + 1) * half]
                if step == 0:
                    dv_s[...] = dv
                    dk_s[...] = dk
                else:
                    dv_s[pl.ds(0, count), :] += dv
                    dk_s[pl.ds(0, count), :] += dk
            for b in range(N_INNER):
                for part in range(2):
                    at = pl.ds(part * side + b * half, half)
                    dkv_ref[b, pl.ds(part * half, half), head] = (dk_s[at, :] * scale).astype(jnp.bfloat16)
                    dkv_ref[b, pl.ds(rows + part * half, half), head] = dv_s[at, :].astype(jnp.bfloat16)

    return pl.pallas_call(
        kernel,
        out_shape=[jax.ShapeDtypeStruct((CHIPS, rows, PAIR), jnp.bfloat16)] * 2
        + [jax.ShapeDtypeStruct(kv.shape, jnp.bfloat16)],
        in_specs=[VMEM] * (3 + CHIPS),
        out_specs=[VMEM] * 3,
        scratch_shapes=[pltpu.VMEM((2 * side, PAIR), jnp.bfloat16)] * 4
        + [pltpu.VMEM((2, 2 * side), jnp.float32)] * 2
        + [pltpu.VMEM((2 * side, WIDTH), jnp.float32)] * 2,
        compiler_params=pltpu.CompilerParams(vmem_limit_bytes=40 * 1024 * 1024),
        name="attend",
    )(kv, kcol, qrow, *parts)


def unpack_q(chunk, parts):
    rows = parts[0].shape[1]

    def kernel(chunk_ref, *rest):
        out = rest[-1]
        for r in range(N_INNER):
            cols = pl.ds(pl.multiple_of(chunk_ref[r] * PAIR, PAIR), PAIR)
            out[:, cols] = rest[r // 2][r % 2].astype(jnp.float32)

    return pl.pallas_call(
        kernel,
        out_shape=jax.ShapeDtypeStruct((rows, N_INNER * PAIR), jnp.float32),
        in_specs=[SMEM] + [VMEM] * CHIPS,
        out_specs=VMEM,
        name="unpack_q",
    )(chunk, *parts)


def unpack_kv(dkv):
    rows = dkv.shape[1] // 2

    def kernel(in_ref, dk_ref, dv_ref):
        for j in range(N_INNER):
            cols = pl.ds(j * PAIR, PAIR)
            dk_ref[:, cols] = in_ref[j, pl.ds(0, rows), :].astype(jnp.float32)
            dv_ref[:, cols] = in_ref[j, pl.ds(rows, rows), :].astype(jnp.float32)

    return pl.pallas_call(
        kernel,
        out_shape=[jax.ShapeDtypeStruct((rows, N_INNER * PAIR), jnp.float32)] * 2,
        in_specs=[VMEM],
        out_specs=[VMEM] * 2,
        name="unpack_kv",
    )(dkv)


def shards(queries, keys, values, grad_out, lse, delta, span_table):
    outer_count = lax.axis_size("outer")
    outer_idx = lax.axis_index("outer")
    inner_idx = lax.axis_index("inner")
    rows = queries.shape[0]
    half = rows // 2
    turns = [(dz, dc) for dz in range(CHIPS) for dc in range(2)]
    chunk = jnp.stack([moved_inner(inner_idx, *t) for t in turns]).astype(jnp.int32)
    senders = jnp.stack([moved_inner(inner_idx, *t, -1) for t in turns]).astype(jnp.int32)

    kv = lax.all_to_all(pack_kv(keys, values), "inner", 0, 0, tiled=True)

    stats = jnp.stack([lse.T.reshape(N_INNER, PAIR), delta.T.reshape(N_INNER, PAIR)], axis=1)
    stats = jnp.pad(stats, ((0, 0), (0, STAT_ROWS - 2), (0, 0)))
    crossed = to_sibling(pack_for_sibling(chunk, queries, grad_out, stats))
    sent = pack_q(chunk, queries, grad_out, stats, crossed)
    axes = ("outer", "inner")
    parts = [lax.ppermute(x, axes, send_pairs(outer_count, dz, False)) for dz, x in enumerate(sent)]

    first = span_table[:, 0].reshape(outer_count, N_INNER)
    key_c = lax.dynamic_index_in_dim(first, outer_idx, 0, keepdims=False)
    query_c = lax.dynamic_index_in_dim(first, (outer_idx + 1) % outer_count, 0, keepdims=False)[senders]
    kcol = jnp.repeat(key_c, half)[:, None]
    qrow = jnp.repeat(query_c, half)[None, :]

    own_dq, sibling_dq, dkv = attend(kv, parts, kcol, qrow)
    dkv = lax.all_to_all(dkv, "inner", 0, 0, tiled=True)
    sent = pack_dq(own_dq, to_sibling(sibling_dq))
    back = [lax.ppermute(x, axes, send_pairs(outer_count, dz, True)) for dz, x in enumerate(sent)]
    grad_k, grad_v = unpack_kv(dkv)
    grad_q = unpack_q(chunk, back)
    return grad_q, grad_k, grad_v


def solution(mesh):
    placed = P(("outer", "inner"), None)
    return jax.shard_map(
        shards,
        mesh=mesh,
        in_specs=(placed,) * 6 + (P(),),
        out_specs=(placed,) * 3,
        check_vma=False,
    )
```

```python
import jax
import jax.numpy as jnp
from jax import lax
from jax.experimental import pallas as pl
from jax.experimental.pallas import tpu as pltpu
from jax.sharding import PartitionSpec as P

N_INNER = 8
WIDTH = 128
PAIR = 2 * WIDTH
STAT_ROWS = 16
LOG2E = 1.4426950408889634
CHIPS = 4
TURNS = (2, 1, 3, 0)
PLANE = 16


def moved_inner(i, dz, dc):
    return ((i // 2 + dz) % CHIPS) * 2 + (i + dc) % 2


def source_turn(o, dz):
    return dz - 1 if o == 0 else dz


def send_pairs(outer_count, dz, back, crossing=True):
    pairs = []
    for o in range(outer_count):
        if o % PLANE == 0 and not crossing:
            continue
        for i in range(N_INNER):
            here = o * N_INNER + i
            there = ((o - 1) % outer_count) * N_INNER + moved_inner(i, source_turn(o, dz), 0)
            pairs.append((there, here) if back else (here, there))
    return pairs


def long_way(outer_count):
    first, second = [], []
    for o in range(0, outer_count, PLANE):
        for i in range(N_INNER):
            far = moved_inner(i, source_turn(o, TURNS[0]), 0)
            middle = o * N_INNER + moved_inner(i, -1, 0)
            first.append((o * N_INNER + i, middle))
            second.append((middle, ((o - 1) % outer_count) * N_INNER + far))
    return first, second


def to_sibling(x):
    return lax.ppermute(x, "inner", [(i, i ^ 1) for i in range(N_INNER)])


VMEM = pl.BlockSpec(memory_space=pltpu.VMEM)
SMEM = pl.BlockSpec(memory_space=pltpu.SMEM)


def pack_kv(keys, values):
    rows = keys.shape[0]

    def kernel(k_ref, v_ref, out_ref):
        for j in range(N_INNER):
            cols = pl.ds(j * PAIR, PAIR)
            out_ref[j, pl.ds(0, rows), :] = k_ref[:, cols]
            out_ref[j, pl.ds(rows, rows), :] = v_ref[:, cols]

    return pl.pallas_call(
        kernel,
        out_shape=jax.ShapeDtypeStruct((N_INNER, 2 * rows, PAIR), keys.dtype),
        in_specs=[VMEM] * 2,
        out_specs=VMEM,
        name="pack_kv",
    )(keys, values)


def chunk_of(q_ref, o_ref, s_ref, j, out, at):
    rows = q_ref.shape[0]
    cols = pl.ds(pl.multiple_of(j * PAIR, PAIR), PAIR)
    out[at + (pl.ds(0, rows), slice(None))] = q_ref[:, cols]
    out[at + (pl.ds(rows, rows), slice(None))] = o_ref[:, cols]
    out[at + (pl.ds(2 * rows, STAT_ROWS), slice(None))] = s_ref[j]


def pack_for_sibling(chunk, queries, grad_out, stats):
    rows = queries.shape[0]

    def kernel(chunk_ref, q_ref, o_ref, s_ref, out_ref):
        for dz in range(CHIPS):
            chunk_of(q_ref, o_ref, s_ref, chunk_ref[2 * dz + 1], out_ref, (dz,))

    return pl.pallas_call(
        kernel,
        out_shape=jax.ShapeDtypeStruct((CHIPS, 2 * rows + STAT_ROWS, PAIR), queries.dtype),
        in_specs=[SMEM] + [VMEM] * 3,
        out_specs=VMEM,
        name="pack_for_sibling",
    )(chunk, queries, grad_out, stats)


def pack_q(chunk, queries, grad_out, stats, from_sibling):
    rows = queries.shape[0]
    whole = 2 * rows + STAT_ROWS

    def kernel(chunk_ref, q_ref, o_ref, s_ref, x_ref, *outs):
        short = outs[0]
        j = chunk_ref[0]
        cols = pl.ds(pl.multiple_of(j * PAIR, PAIR), PAIR)
        short[pl.ds(0, rows), :] = q_ref[:, cols]
        short[pl.ds(rows, STAT_ROWS), :] = s_ref[j]
        short[pl.ds(rows + STAT_ROWS, whole), :] = x_ref[0]
        for t in range(1, CHIPS):
            chunk_of(q_ref, o_ref, s_ref, chunk_ref[2 * t], outs[t], (0,))
            outs[t][1] = x_ref[t]

    return pl.pallas_call(
        kernel,
        out_shape=[jax.ShapeDtypeStruct((rows + STAT_ROWS + whole, PAIR), queries.dtype)]
        + [jax.ShapeDtypeStruct((2, whole, PAIR), queries.dtype)] * (CHIPS - 1),
        in_specs=[SMEM] + [VMEM] * 4,
        out_specs=[VMEM] * CHIPS,
        name="pack_q",
    )(chunk, queries, grad_out, stats, from_sibling)


def pack_dq(own, from_sibling):
    def kernel(own_ref, x_ref, *outs):
        for t, out in enumerate(outs):
            out[0] = own_ref[t]
            out[1] = x_ref[t]

    return pl.pallas_call(
        kernel,
        out_shape=[jax.ShapeDtypeStruct((2,) + own.shape[1:], own.dtype)] * CHIPS,
        in_specs=[VMEM] * 2,
        out_specs=[VMEM] * CHIPS,
        name="pack_dq",
    )(own, from_sibling)


def attend(kv, parts, slice_o, kcol, qrow):
    rows = kv.shape[1] // 2
    half = rows // 2
    side = N_INNER * half
    scale = WIDTH ** -0.5
    tile = 256

    def kernel(kv_ref, kcol_ref, qrow_ref, slice_ref, *rest):
        ins, rest = rest[:CHIPS], rest[CHIPS:]
        from_start = (0, rows, 2 * rows)
        blocks = [(ins[a // 2].at[a % 2], from_start) for a in range(2, N_INNER)]
        after = rows + STAT_ROWS
        blocks = [(ins[0], (0, None, rows)), (ins[0], tuple(after + r for r in from_start))] + blocks
        dqs = [rest[a % 2].at[a // 2] for a in range(N_INNER)]
        dkv_ref, q_s, o_s, k_s, v_s, l_s, d_s, dk_s, dv_s = rest[2:]
        for a in range(N_INNER):
            ref, (q_at, o_at, s_at) = blocks[a]
            for part in range(2):
                to = pl.ds(part * side + a * half, half)
                at = part * half
                q_s[to, :] = ref[pl.ds(q_at + at, half), :]
                if o_at is None:
                    o_s[to, :] = slice_ref[pl.ds(at, half), :]
                else:
                    o_s[to, :] = ref[pl.ds(o_at + at, half), :]
                k_s[to, :] = kv_ref[a, pl.ds(at, half), :]
                v_s[to, :] = kv_ref[a, pl.ds(rows + at, half), :]
            st = ref[pl.ds(s_at, STAT_ROWS), :].astype(jnp.float32)
            for h in range(2):
                for part in range(2):
                    lanes = slice(h * WIDTH + part * half, h * WIDTH + (part + 1) * half)
                    to = pl.ds(part * side + a * half, half)
                    l_s[pl.ds(h, 1), to] = st[0:1, lanes] * LOG2E
                    d_s[pl.ds(h, 1), to] = st[1:2, lanes]
        nt = (((1,), (1,)), ((), ()))
        f32 = jnp.float32
        for h in range(2):
            head = pl.ds(h * WIDTH, WIDTH)
            k_all = k_s[:, head]
            v_all = v_s[:, head]
            kt = k_all.astype(f32).T.astype(jnp.bfloat16)
            for step, (part, piece) in enumerate(((1, 0), (1, 1), (0, 0), (0, 1))):
                qs = pl.ds(part * side + piece * tile, tile)
                q = q_s[qs, head]
                o = o_s[qs, head]
                count = 2 * side if part else side
                l = l_s[pl.ds(h, 1), qs]
                d = d_s[pl.ds(h, 1), qs]
                s = lax.dot_general(k_all[:count], q, nt, preferred_element_type=f32)
                p = jnp.exp2(s * (scale * LOG2E) - l)
                qc = qrow_ref[:, pl.ds(piece * tile, tile)]
                if part:
                    p = jnp.concatenate([p[:side], jnp.where(kcol_ref[...] > qc, p[side:], 0.0)], 0)
                else:
                    p = jnp.where(kcol_ref[...] < qc, p, 0.0)
                dp = lax.dot_general(v_all[:count], o, nt, preferred_element_type=f32)
                ds = (p * (dp - d)).astype(jnp.bfloat16)
                dv = jnp.dot(p.astype(jnp.bfloat16), o, preferred_element_type=f32)
                dk = jnp.dot(ds, q, preferred_element_type=f32)
                dqt = jnp.dot(kt[:, :count], ds, preferred_element_type=f32)
                dq = (dqt * scale).T.astype(jnp.bfloat16)
                per = tile // half
                for a in range(per):
                    dqs[piece * per + a][pl.ds(part * half, half), head] = dq[a * half:(a + 1) * half]
                if step == 0:
                    dv_s[...] = dv
                    dk_s[...] = dk
                else:
                    dv_s[pl.ds(0, count), :] += dv
                    dk_s[pl.ds(0, count), :] += dk
            for b in range(N_INNER):
                for part in range(2):
                    at = pl.ds(part * side + b * half, half)
                    dkv_ref[b, pl.ds(part * half, half), head] = (dk_s[at, :] * scale).astype(jnp.bfloat16)
                    dkv_ref[b, pl.ds(rows + part * half, half), head] = dv_s[at, :].astype(jnp.bfloat16)

    return pl.pallas_call(
        kernel,
        out_shape=[jax.ShapeDtypeStruct((CHIPS, rows, PAIR), jnp.bfloat16)] * 2
        + [jax.ShapeDtypeStruct(kv.shape, jnp.bfloat16)],
        in_specs=[VMEM] * (4 + CHIPS),
        out_specs=[VMEM] * 3,
        scratch_shapes=[pltpu.VMEM((2 * side, PAIR), jnp.bfloat16)] * 4
        + [pltpu.VMEM((2, 2 * side), jnp.float32)] * 2
        + [pltpu.VMEM((2 * side, WIDTH), jnp.float32)] * 2,
        compiler_params=pltpu.CompilerParams(vmem_limit_bytes=40 * 1024 * 1024),
        name="attend",
    )(kv, kcol, qrow, slice_o, *parts)


def unpack_q(chunk, parts):
    rows = parts[0].shape[1]

    def kernel(chunk_ref, *rest):
        out = rest[-1]
        for r in range(N_INNER):
            cols = pl.ds(pl.multiple_of(chunk_ref[r] * PAIR, PAIR), PAIR)
            out[:, cols] = rest[r // 2][r % 2].astype(jnp.float32)

    return pl.pallas_call(
        kernel,
        out_shape=jax.ShapeDtypeStruct((rows, N_INNER * PAIR), jnp.float32),
        in_specs=[SMEM] + [VMEM] * CHIPS,
        out_specs=VMEM,
        name="unpack_q",
    )(chunk, *parts)


def unpack_kv(dkv):
    rows = dkv.shape[1] // 2

    def kernel(in_ref, dk_ref, dv_ref):
        for j in range(N_INNER):
            cols = pl.ds(j * PAIR, PAIR)
            dk_ref[:, cols] = in_ref[j, pl.ds(0, rows), :].astype(jnp.float32)
            dv_ref[:, cols] = in_ref[j, pl.ds(rows, rows), :].astype(jnp.float32)

    return pl.pallas_call(
        kernel,
        out_shape=[jax.ShapeDtypeStruct((rows, N_INNER * PAIR), jnp.float32)] * 2,
        in_specs=[VMEM],
        out_specs=[VMEM] * 2,
        name="unpack_kv",
    )(dkv)


def shards(queries, keys, values, grad_out, lse, delta, span_table):
    outer_count = lax.axis_size("outer")
    outer_idx = lax.axis_index("outer")
    inner_idx = lax.axis_index("inner")
    rows = queries.shape[0]
    half = rows // 2
    to_wrap = (outer_idx == 0).astype(jnp.int32)
    from_wrap = (outer_idx == outer_count - 1).astype(jnp.int32)
    chunk = jnp.stack([moved_inner(inner_idx, dz - to_wrap, dc) for dz in TURNS for dc in range(2)])
    senders = jnp.stack([moved_inner(inner_idx, from_wrap - dz, dc) for dz in TURNS for dc in range(2)])

    axes = ("outer", "inner")
    first_leg, second_leg = long_way(outer_count)

    kv = lax.all_to_all(pack_kv(keys, values), "inner", 0, 0, tiled=True)

    slice_o = lax.dynamic_slice_in_dim(grad_out, chunk[0] * PAIR, PAIR, 1)
    middle = lax.ppermute(slice_o, axes, first_leg)
    slice_o = jnp.where(outer_idx % PLANE == 0, middle, slice_o)

    stats = jnp.stack([lse.T.reshape(N_INNER, PAIR), delta.T.reshape(N_INNER, PAIR)], axis=1)
    stats = jnp.pad(stats, ((0, 0), (0, STAT_ROWS - 2), (0, 0)))
    crossed = to_sibling(pack_for_sibling(chunk, queries, grad_out, stats))
    sent = pack_q(chunk, queries, grad_out, stats, crossed)
    slice_o = lax.ppermute(slice_o, axes, send_pairs(outer_count, TURNS[0], False, crossing=False) + second_leg)
    parts = [lax.ppermute(x, axes, send_pairs(outer_count, dz, False)) for dz, x in zip(TURNS, sent)]

    first = span_table[:, 0].reshape(outer_count, N_INNER)
    key_c = lax.dynamic_index_in_dim(first, outer_idx, 0, keepdims=False)
    query_c = lax.dynamic_index_in_dim(first, (outer_idx + 1) % outer_count, 0, keepdims=False)[senders]
    kcol = jnp.repeat(key_c, half)[:, None]
    qrow = jnp.repeat(query_c, half)[None, :]

    own_dq, sibling_dq, dkv = attend(kv, parts, slice_o, kcol, qrow)
    dkv = lax.all_to_all(dkv, "inner", 0, 0, tiled=True)
    sent = pack_dq(own_dq, to_sibling(sibling_dq))
    back = [lax.ppermute(x, axes, send_pairs(outer_count, dz, True)) for dz, x in zip(TURNS, sent)]
    grad_k, grad_v = unpack_kv(dkv)
    back, grad_k, grad_v = lax.optimization_barrier((back, grad_k, grad_v))
    grad_q = unpack_q(chunk, back)
    return grad_q, grad_k, grad_v


def solution(mesh):
    placed = P(("outer", "inner"), None)
    return jax.shard_map(
        shards,
        mesh=mesh,
        in_specs=(placed,) * 6 + (P(),),
        out_specs=(placed,) * 3,
        check_vma=False,
    )
```

```python
import jax
import jax.numpy as jnp
from jax import lax
from jax.experimental import pallas as pl
from jax.experimental.pallas import tpu as pltpu
from jax.sharding import PartitionSpec as P

N_INNER = 8
WIDTH = 128
PAIR = 2 * WIDTH
STAT_ROWS = 16
LOG2E = 1.4426950408889634
CHIPS = 4
TURNS = (2, 1, 3, 0)
PLANE = 16


def moved_inner(i, dz, dc):
    return ((i // 2 + dz) % CHIPS) * 2 + (i + dc) % 2


def source_turn(o, dz):
    return dz - 1 if o == 0 else dz


def send_pairs(outer_count, dz, back, crossing=True):
    pairs = []
    for o in range(outer_count):
        if o % PLANE == 0 and not crossing:
            continue
        for i in range(N_INNER):
            here = o * N_INNER + i
            there = ((o - 1) % outer_count) * N_INNER + moved_inner(i, source_turn(o, dz), 0)
            pairs.append((there, here) if back else (here, there))
    return pairs


def long_way(outer_count, back):
    first, second = [], []
    planes = outer_count // PLANE
    for o in range(0, outer_count, PLANE):
        owner = (o - 1) % outer_count
        for i in range(N_INNER):
            far = moved_inner(i, source_turn(o, TURNS[0]), 0)
            here, there = o * N_INNER + i, owner * N_INNER + far
            if back:
                z = (far // 2 * planes + owner // PLANE + 2) % (planes * CHIPS)
                middle = (z % planes * PLANE + PLANE - 1) * N_INNER + z // planes * 2 + far % 2
                here, there = there, here
            else:
                z = (i // 2 * planes + o // PLANE - 2) % (planes * CHIPS)
                middle = z % planes * PLANE * N_INNER + z // planes * 2 + i % 2
            first.append((here, middle))
            second.append((middle, there))
    return first, second


def to_sibling(x):
    return lax.ppermute(x, "inner", [(i, i ^ 1) for i in range(N_INNER)])


VMEM = pl.BlockSpec(memory_space=pltpu.VMEM)
SMEM = pl.BlockSpec(memory_space=pltpu.SMEM)


def pack_kv(keys, values):
    rows = keys.shape[0]

    def kernel(k_ref, v_ref, out_ref):
        for j in range(N_INNER):
            cols = pl.ds(j * PAIR, PAIR)
            out_ref[j, pl.ds(0, rows), :] = k_ref[:, cols]
            out_ref[j, pl.ds(rows, rows), :] = v_ref[:, cols]

    return pl.pallas_call(
        kernel,
        out_shape=jax.ShapeDtypeStruct((N_INNER, 2 * rows, PAIR), keys.dtype),
        in_specs=[VMEM] * 2,
        out_specs=VMEM,
        name="pack_kv",
    )(keys, values)


def chunk_of(q_ref, o_ref, s_ref, j, out, at):
    rows = q_ref.shape[0]
    cols = pl.ds(pl.multiple_of(j * PAIR, PAIR), PAIR)
    out[at + (pl.ds(0, rows), slice(None))] = q_ref[:, cols]
    out[at + (pl.ds(rows, rows), slice(None))] = o_ref[:, cols]
    out[at + (pl.ds(2 * rows, STAT_ROWS), slice(None))] = s_ref[j]


def pack_for_sibling(chunk, queries, grad_out, stats):
    rows = queries.shape[0]

    def kernel(chunk_ref, q_ref, o_ref, s_ref, out_ref):
        for dz in range(CHIPS):
            chunk_of(q_ref, o_ref, s_ref, chunk_ref[2 * dz + 1], out_ref, (dz,))

    return pl.pallas_call(
        kernel,
        out_shape=jax.ShapeDtypeStruct((CHIPS, 2 * rows + STAT_ROWS, PAIR), queries.dtype),
        in_specs=[SMEM] + [VMEM] * 3,
        out_specs=VMEM,
        name="pack_for_sibling",
    )(chunk, queries, grad_out, stats)


def pack_q(chunk, queries, grad_out, stats, from_sibling):
    rows = queries.shape[0]

    def kernel(chunk_ref, q_ref, o_ref, s_ref, x_ref, *outs):
        for t, out in enumerate(outs):
            j = chunk_ref[2 * t]
            cols = pl.ds(pl.multiple_of(j * PAIR, PAIR), PAIR)
            out[pl.ds(0, rows), :] = q_ref[:, cols]
            if t:
                out[pl.ds(rows, rows), :] = o_ref[:, cols]
            at = 2 * rows if t else rows
            out[pl.ds(at, 2 * rows), :] = x_ref[t, pl.ds(0, 2 * rows), :]
            both = s_ref[j].astype(jnp.float32) + x_ref[t, pl.ds(2 * rows, STAT_ROWS), :].astype(jnp.float32)
            out[pl.ds(at + 2 * rows, STAT_ROWS), :] = both.astype(out.dtype)

    return pl.pallas_call(
        kernel,
        out_shape=[
            jax.ShapeDtypeStruct(((4 if t else 3) * rows + STAT_ROWS, PAIR), queries.dtype) for t in range(CHIPS)
        ],
        in_specs=[SMEM] + [VMEM] * 4,
        out_specs=[VMEM] * CHIPS,
        name="pack_q",
    )(chunk, queries, grad_out, stats, from_sibling)


def pack_dq(own, from_sibling):
    rows = own.shape[1]
    kept = rows - rows // 4

    def kernel(own_ref, x_ref, *outs):
        outs[0][pl.ds(0, kept), :] = own_ref[0, pl.ds(0, kept), :]
        outs[0][pl.ds(kept, rows), :] = x_ref[0]
        for t in range(1, CHIPS):
            outs[t][0] = own_ref[t]
            outs[t][1] = x_ref[t]

    return pl.pallas_call(
        kernel,
        out_shape=[jax.ShapeDtypeStruct((kept + rows, PAIR), own.dtype)]
        + [jax.ShapeDtypeStruct((2,) + own.shape[1:], own.dtype)] * (CHIPS - 1),
        in_specs=[VMEM] * 2,
        out_specs=[VMEM] * CHIPS,
        cost_estimate=pl.CostEstimate(flops=40 * 10**9, bytes_accessed=2**20, transcendentals=0),
        name="pack_dq",
    )(own, from_sibling)


def attend(kv, parts, slice_o, kcol, qrow):
    rows = kv.shape[1] // 2
    half = rows // 2
    side = N_INNER * half
    scale = WIDTH ** -0.5
    tile = 256

    def kernel(kv_ref, kcol_ref, qrow_ref, slice_ref, *rest):
        ins, rest = rest[:CHIPS], rest[CHIPS:]
        blocks = [(0, None), (rows, 2 * rows)] + [(0, rows), (2 * rows, 3 * rows)] * (CHIPS - 1)
        dqs = [rest[a % 2].at[a // 2] for a in range(N_INNER)]
        slice_dq, dkv_ref, q_s, o_s, k_s, v_s, l_s, d_s, dk_s, dv_s = rest[2:]
        for a in range(N_INNER):
            ref, (q_at, o_at) = ins[a // 2], blocks[a]
            for part in range(2):
                to = pl.ds(part * side + a * half, half)
                at = part * half
                q_s[to, :] = ref[pl.ds(q_at + at, half), :]
                if o_at is None:
                    o_s[to, :] = slice_ref[pl.ds(at, half), :]
                else:
                    o_s[to, :] = ref[pl.ds(o_at + at, half), :]
                k_s[to, :] = kv_ref[a, pl.ds(at, half), :]
                v_s[to, :] = kv_ref[a, pl.ds(rows + at, half), :]
            st = ref[pl.ds(ref.shape[0] - STAT_ROWS, STAT_ROWS), :].astype(jnp.float32)
            row = 2 * (a % 2)
            for h in range(2):
                for part in range(2):
                    lanes = slice(h * WIDTH + part * half, h * WIDTH + (part + 1) * half)
                    to = pl.ds(part * side + a * half, half)
                    l_s[pl.ds(h, 1), to] = st[row:row + 1, lanes] * LOG2E
                    d_s[pl.ds(h, 1), to] = st[row + 1:row + 2, lanes]
        nt = (((1,), (1,)), ((), ()))
        f32 = jnp.float32
        for h in range(2):
            head = pl.ds(h * WIDTH, WIDTH)
            k_all = k_s[:, head]
            v_all = v_s[:, head]
            kt = k_all.astype(f32).T.astype(jnp.bfloat16)
            for step, (part, piece) in enumerate(((1, 0), (1, 1), (0, 0), (0, 1))):
                qs = pl.ds(part * side + piece * tile, tile)
                q = q_s[qs, head]
                o = o_s[qs, head]
                count = 2 * side if part else side
                l = l_s[pl.ds(h, 1), qs]
                d = d_s[pl.ds(h, 1), qs]
                s = lax.dot_general(k_all[:count], q, nt, preferred_element_type=f32)
                p = jnp.exp2(s * (scale * LOG2E) - l)
                qc = qrow_ref[:, pl.ds(piece * tile, tile)]
                if part:
                    p = jnp.concatenate([p[:side], jnp.where(kcol_ref[...] > qc, p[side:], 0.0)], 0)
                else:
                    p = jnp.where(kcol_ref[...] < qc, p, 0.0)
                dp = lax.dot_general(v_all[:count], o, nt, preferred_element_type=f32)
                ds = (p * (dp - d)).astype(jnp.bfloat16)
                dv = jnp.dot(p.astype(jnp.bfloat16), o, preferred_element_type=f32)
                dk = jnp.dot(ds, q, preferred_element_type=f32)
                dqt = jnp.dot(kt[:, :count], ds, preferred_element_type=f32)
                dq = (dqt * scale).T.astype(jnp.bfloat16)
                per = tile // half
                for a in range(per):
                    dqs[piece * per + a][pl.ds(part * half, half), head] = dq[a * half:(a + 1) * half]
                if part and piece == 0:
                    slice_dq[:, head] = dq[half // 2:half]
                if step == 0:
                    dv_s[...] = dv
                    dk_s[...] = dk
                else:
                    dv_s[pl.ds(0, count), :] += dv
                    dk_s[pl.ds(0, count), :] += dk
            for b in range(N_INNER):
                for part in range(2):
                    at = pl.ds(part * side + b * half, half)
                    dkv_ref[b, pl.ds(part * half, half), head] = (dk_s[at, :] * scale).astype(jnp.bfloat16)
                    dkv_ref[b, pl.ds(rows + part * half, half), head] = dv_s[at, :].astype(jnp.bfloat16)

    return pl.pallas_call(
        kernel,
        out_shape=[jax.ShapeDtypeStruct((CHIPS, rows, PAIR), jnp.bfloat16)] * 2
        + [jax.ShapeDtypeStruct((half // 2, PAIR), jnp.bfloat16), jax.ShapeDtypeStruct(kv.shape, jnp.bfloat16)],
        in_specs=[VMEM] * (4 + CHIPS),
        out_specs=[VMEM] * 4,
        scratch_shapes=[pltpu.VMEM((2 * side, PAIR), jnp.bfloat16)] * 4
        + [pltpu.VMEM((2, 2 * side), jnp.float32)] * 2
        + [pltpu.VMEM((2 * side, WIDTH), jnp.float32)] * 2,
        compiler_params=pltpu.CompilerParams(vmem_limit_bytes=40 * 1024 * 1024),
        name="attend",
    )(kv, kcol, qrow, slice_o, *parts)


def unpack_q(chunk, slice_dq, parts):
    rows = parts[1].shape[1]
    kept = rows - slice_dq.shape[0]

    def kernel(chunk_ref, slice_ref, *rest):
        out = rest[-1]
        cols = [pl.ds(pl.multiple_of(chunk_ref[r] * PAIR, PAIR), PAIR) for r in range(N_INNER)]
        out[pl.ds(0, kept), cols[0]] = rest[0][pl.ds(0, kept), :].astype(jnp.float32)
        out[pl.ds(kept, rows - kept), cols[0]] = slice_ref[...].astype(jnp.float32)
        out[:, cols[1]] = rest[0][pl.ds(kept, rows), :].astype(jnp.float32)
        for r in range(2, N_INNER):
            out[:, cols[r]] = rest[r // 2][r % 2].astype(jnp.float32)

    return pl.pallas_call(
        kernel,
        out_shape=jax.ShapeDtypeStruct((rows, N_INNER * PAIR), jnp.float32),
        in_specs=[SMEM] + [VMEM] * (1 + CHIPS),
        out_specs=VMEM,
        name="unpack_q",
    )(chunk, slice_dq, *parts)


def unpack_kv(dkv):
    rows = dkv.shape[1] // 2

    def kernel(in_ref, dk_ref, dv_ref):
        for j in range(N_INNER):
            cols = pl.ds(j * PAIR, PAIR)
            dk_ref[:, cols] = in_ref[j, pl.ds(0, rows), :].astype(jnp.float32)
            dv_ref[:, cols] = in_ref[j, pl.ds(rows, rows), :].astype(jnp.float32)

    return pl.pallas_call(
        kernel,
        out_shape=[jax.ShapeDtypeStruct((rows, N_INNER * PAIR), jnp.float32)] * 2,
        in_specs=[VMEM],
        out_specs=[VMEM] * 2,
        name="unpack_kv",
    )(dkv)


def shards(queries, keys, values, grad_out, lse, delta, span_table):
    outer_count = lax.axis_size("outer")
    outer_idx = lax.axis_index("outer")
    inner_idx = lax.axis_index("inner")
    rows = queries.shape[0]
    half = rows // 2
    to_wrap = (outer_idx == 0).astype(jnp.int32)
    from_wrap = (outer_idx == outer_count - 1).astype(jnp.int32)
    chunk = jnp.stack([moved_inner(inner_idx, dz - to_wrap, dc) for dz in TURNS for dc in range(2)])
    senders = jnp.stack([moved_inner(inner_idx, from_wrap - dz, dc) for dz in TURNS for dc in range(2)])

    axes = ("outer", "inner")
    first_leg, second_leg = long_way(outer_count, False)

    kv = lax.all_to_all(pack_kv(keys, values), "inner", 0, 0, tiled=True)

    slice_o = lax.dynamic_slice_in_dim(grad_out, chunk[0] * PAIR, PAIR, 1)
    middle = lax.ppermute(slice_o, axes, first_leg)
    slice_o = jnp.where(outer_idx % PLANE == 0, middle, slice_o)

    stats = jnp.stack([lse.T.reshape(N_INNER, PAIR), delta.T.reshape(N_INNER, PAIR)], axis=1)
    own_stats = jnp.pad(stats, ((0, 0), (0, STAT_ROWS - 2), (0, 0)))
    stats = jnp.pad(stats, ((0, 0), (2, STAT_ROWS - 4), (0, 0)))
    crossed = to_sibling(pack_for_sibling(chunk, queries, grad_out, stats))
    sent = pack_q(chunk, queries, grad_out, own_stats, crossed)
    slice_o = lax.ppermute(slice_o, axes, send_pairs(outer_count, TURNS[0], False, crossing=False) + second_leg)
    parts = [lax.ppermute(x, axes, send_pairs(outer_count, dz, False)) for dz, x in zip(TURNS, sent)]

    first = span_table[:, 0].reshape(outer_count, N_INNER)
    key_c = lax.dynamic_index_in_dim(first, outer_idx, 0, keepdims=False)
    query_c = lax.dynamic_index_in_dim(first, (outer_idx + 1) % outer_count, 0, keepdims=False)[senders]
    kcol = jnp.repeat(key_c, half)[:, None]
    qrow = jnp.repeat(query_c, half)[None, :]

    own_dq, sibling_dq, slice_dq, dkv = attend(kv, parts, slice_o, kcol, qrow)
    dkv = lax.all_to_all(dkv, "inner", 0, 0, tiled=True)
    first_leg, second_leg = long_way(outer_count, True)
    middle = lax.ppermute(slice_dq, axes, first_leg)
    sent = pack_dq(own_dq, to_sibling(sibling_dq))
    back = [lax.ppermute(x, axes, send_pairs(outer_count, dz, True)) for dz, x in zip(TURNS, sent)]
    slice_dq = jnp.where(outer_idx % PLANE == PLANE - 1, middle, slice_dq)
    slice_dq = lax.ppermute(slice_dq, axes, send_pairs(outer_count, TURNS[0], True, crossing=False) + second_leg)
    grad_k, grad_v = unpack_kv(dkv)
    back, grad_k, grad_v = lax.optimization_barrier((back, grad_k, grad_v))
    grad_q = unpack_q(chunk, slice_dq, back)
    return grad_q, grad_k, grad_v


def solution(mesh):
    placed = P(("outer", "inner"), None)
    return jax.shard_map(
        shards,
        mesh=mesh,
        in_specs=(placed,) * 6 + (P(),),
        out_specs=(placed,) * 3,
        check_vma=False,
    )
```

```python
import jax
import jax.numpy as jnp
from jax import lax
from jax.experimental import pallas as pl
from jax.experimental.pallas import tpu as pltpu
from jax.sharding import PartitionSpec as P

N_INNER = 8
WIDTH = 128
PAIR = 2 * WIDTH
STAT_ROWS = 16
LOG2E = 1.4426950408889634
CHIPS = 4
TURNS = (2, 1, 3, 0)
PLANE = 16


def moved_inner(i, dz, dc):
    return ((i // 2 + dz) % CHIPS) * 2 + (i + dc) % 2


def source_turn(o, dz):
    return dz - 1 if o == 0 else dz


def send_pairs(outer_count, dz, back, crossing=True):
    pairs = []
    for o in range(outer_count):
        if o % PLANE == 0 and not crossing:
            continue
        for i in range(N_INNER):
            here = o * N_INNER + i
            there = ((o - 1) % outer_count) * N_INNER + moved_inner(i, source_turn(o, dz), 0)
            pairs.append((there, here) if back else (here, there))
    return pairs


def long_way(outer_count, back):
    first, second = [], []
    planes = outer_count // PLANE
    for o in range(0, outer_count, PLANE):
        owner = (o - 1) % outer_count
        for i in range(N_INNER):
            far = moved_inner(i, source_turn(o, TURNS[0]), 0)
            here, there = o * N_INNER + i, owner * N_INNER + far
            if back:
                z = (far // 2 * planes + owner // PLANE + 2) % (planes * CHIPS)
                middle = (z % planes * PLANE + PLANE - 1) * N_INNER + z // planes * 2 + far % 2
                here, there = there, here
            else:
                z = (i // 2 * planes + o // PLANE - 2) % (planes * CHIPS)
                middle = z % planes * PLANE * N_INNER + z // planes * 2 + i % 2
            first.append((here, middle))
            second.append((middle, there))
    return first, second


def to_sibling(x):
    return lax.ppermute(x, "inner", [(i, i ^ 1) for i in range(N_INNER)])


VMEM = pl.BlockSpec(memory_space=pltpu.VMEM)
SMEM = pl.BlockSpec(memory_space=pltpu.SMEM)


def pack_kv(keys, values):
    rows = keys.shape[0]

    def kernel(k_ref, v_ref, out_ref):
        for j in range(N_INNER):
            cols = pl.ds(j * PAIR, PAIR)
            out_ref[j, pl.ds(0, rows), :] = k_ref[:, cols]
            out_ref[j, pl.ds(rows, rows), :] = v_ref[:, cols]

    return pl.pallas_call(
        kernel,
        out_shape=jax.ShapeDtypeStruct((N_INNER, 2 * rows, PAIR), keys.dtype),
        in_specs=[VMEM] * 2,
        out_specs=VMEM,
        name="pack_kv",
    )(keys, values)


def chunk_of(q_ref, o_ref, s_ref, j, out, at):
    rows = q_ref.shape[0]
    cols = pl.ds(pl.multiple_of(j * PAIR, PAIR), PAIR)
    out[at + (pl.ds(0, rows), slice(None))] = q_ref[:, cols]
    out[at + (pl.ds(rows, rows), slice(None))] = o_ref[:, cols]
    out[at + (pl.ds(2 * rows, STAT_ROWS), slice(None))] = s_ref[j]


def pack_for_sibling(chunk, queries, grad_out, stats):
    rows = queries.shape[0]

    def kernel(chunk_ref, q_ref, o_ref, s_ref, out_ref):
        for dz in range(CHIPS):
            chunk_of(q_ref, o_ref, s_ref, chunk_ref[2 * dz + 1], out_ref, (dz,))

    return pl.pallas_call(
        kernel,
        out_shape=jax.ShapeDtypeStruct((CHIPS, 2 * rows + STAT_ROWS, PAIR), queries.dtype),
        in_specs=[SMEM] + [VMEM] * 3,
        out_specs=VMEM,
        name="pack_for_sibling",
    )(chunk, queries, grad_out, stats)


def pack_q(chunk, queries, grad_out, stats, from_sibling):
    rows = queries.shape[0]

    def kernel(chunk_ref, q_ref, o_ref, s_ref, x_ref, *outs):
        for t, out in enumerate(outs):
            j = chunk_ref[2 * t]
            cols = pl.ds(pl.multiple_of(j * PAIR, PAIR), PAIR)
            out[pl.ds(0, rows), :] = q_ref[:, cols]
            if t:
                out[pl.ds(rows, rows), :] = o_ref[:, cols]
            at = 2 * rows if t else rows
            out[pl.ds(at, 2 * rows), :] = x_ref[t, pl.ds(0, 2 * rows), :]
            both = s_ref[j].astype(jnp.float32) + x_ref[t, pl.ds(2 * rows, STAT_ROWS), :].astype(jnp.float32)
            out[pl.ds(at + 2 * rows, STAT_ROWS), :] = both.astype(out.dtype)

    return pl.pallas_call(
        kernel,
        out_shape=[
            jax.ShapeDtypeStruct(((4 if t else 3) * rows + STAT_ROWS, PAIR), queries.dtype) for t in range(CHIPS)
        ],
        in_specs=[SMEM] + [VMEM] * 4,
        out_specs=[VMEM] * CHIPS,
        name="pack_q",
    )(chunk, queries, grad_out, stats, from_sibling)


def pack_dq(own, from_sibling):
    rows = own.shape[1]
    kept = rows - rows // 4

    def kernel(own_ref, x_ref, *outs):
        outs[0][pl.ds(0, kept), :] = own_ref[0, pl.ds(0, kept), :]
        outs[0][pl.ds(kept, rows), :] = x_ref[0]
        for t in range(1, CHIPS):
            outs[t][0] = own_ref[t]
            outs[t][1] = x_ref[t]

    return pl.pallas_call(
        kernel,
        out_shape=[jax.ShapeDtypeStruct((kept + rows, PAIR), own.dtype)]
        + [jax.ShapeDtypeStruct((2,) + own.shape[1:], own.dtype)] * (CHIPS - 1),
        in_specs=[VMEM] * 2,
        out_specs=[VMEM] * CHIPS,
        cost_estimate=pl.CostEstimate(flops=4 * 10**9, bytes_accessed=2**20, transcendentals=0),
        name="pack_dq",
    )(own, from_sibling)


def attend(kv, parts, slice_o, kcol, qrow):
    rows = kv.shape[1] // 2
    half = rows // 2
    side = N_INNER * half
    scale = WIDTH ** -0.5
    tile = 256

    def kernel(kv_ref, kcol_ref, qrow_ref, slice_ref, *rest):
        ins, rest = rest[:CHIPS], rest[CHIPS:]
        blocks = [(0, None), (rows, 2 * rows)] + [(0, rows), (2 * rows, 3 * rows)] * (CHIPS - 1)
        dqs = [rest[a % 2].at[a // 2] for a in range(N_INNER)]
        slice_dq, dkv_ref, q_s, o_s, k_s, v_s, l_s, d_s, dk_s, dv_s = rest[2:]
        for a in range(N_INNER):
            ref, (q_at, o_at) = ins[a // 2], blocks[a]
            for part in range(2):
                to = pl.ds(part * side + a * half, half)
                at = part * half
                q_s[to, :] = ref[pl.ds(q_at + at, half), :]
                if o_at is None:
                    o_s[to, :] = slice_ref[pl.ds(at, half), :]
                else:
                    o_s[to, :] = ref[pl.ds(o_at + at, half), :]
                k_s[to, :] = kv_ref[a, pl.ds(at, half), :]
                v_s[to, :] = kv_ref[a, pl.ds(rows + at, half), :]
            st = ref[pl.ds(ref.shape[0] - STAT_ROWS, STAT_ROWS), :].astype(jnp.float32)
            row = 2 * (a % 2)
            for h in range(2):
                for part in range(2):
                    lanes = slice(h * WIDTH + part * half, h * WIDTH + (part + 1) * half)
                    to = pl.ds(part * side + a * half, half)
                    l_s[pl.ds(h, 1), to] = st[row:row + 1, lanes] * LOG2E
                    d_s[pl.ds(h, 1), to] = st[row + 1:row + 2, lanes]
        nt = (((1,), (1,)), ((), ()))
        f32 = jnp.float32
        for h in range(2):
            head = pl.ds(h * WIDTH, WIDTH)
            k_all = k_s[:, head]
            v_all = v_s[:, head]
            kt = k_all.astype(f32).T.astype(jnp.bfloat16)
            for step, (part, piece) in enumerate(((1, 0), (1, 1), (0, 0), (0, 1))):
                qs = pl.ds(part * side + piece * tile, tile)
                q = q_s[qs, head]
                o = o_s[qs, head]
                count = 2 * side if part else side
                l = l_s[pl.ds(h, 1), qs]
                d = d_s[pl.ds(h, 1), qs]
                s = lax.dot_general(k_all[:count], q, nt, preferred_element_type=f32)
                p = jnp.exp2(s * (scale * LOG2E) - l)
                qc = qrow_ref[:, pl.ds(piece * tile, tile)]
                if part:
                    p = jnp.concatenate([p[:side], jnp.where(kcol_ref[...] > qc, p[side:], 0.0)], 0)
                else:
                    p = jnp.where(kcol_ref[...] < qc, p, 0.0)
                dp = lax.dot_general(v_all[:count], o, nt, preferred_element_type=f32)
                ds = (p * (dp - d)).astype(jnp.bfloat16)
                dv = jnp.dot(p.astype(jnp.bfloat16), o, preferred_element_type=f32)
                dk = jnp.dot(ds, q, preferred_element_type=f32)
                dqt = jnp.dot(kt[:, :count], ds, preferred_element_type=f32)
                dq = (dqt * scale).T.astype(jnp.bfloat16)
                per = tile // half
                for a in range(per):
                    dqs[piece * per + a][pl.ds(part * half, half), head] = dq[a * half:(a + 1) * half]
                if part and piece == 0:
                    slice_dq[:, head] = dq[half // 2:half]
                if step == 0:
                    dv_s[...] = dv
                    dk_s[...] = dk
                else:
                    dv_s[pl.ds(0, count), :] += dv
                    dk_s[pl.ds(0, count), :] += dk
            for b in range(N_INNER):
                for part in range(2):
                    at = pl.ds(part * side + b * half, half)
                    dkv_ref[b, pl.ds(part * half, half), head] = (dk_s[at, :] * scale).astype(jnp.bfloat16)
                    dkv_ref[b, pl.ds(rows + part * half, half), head] = dv_s[at, :].astype(jnp.bfloat16)

    return pl.pallas_call(
        kernel,
        out_shape=[jax.ShapeDtypeStruct((CHIPS, rows, PAIR), jnp.bfloat16)] * 2
        + [jax.ShapeDtypeStruct((half // 2, PAIR), jnp.bfloat16), jax.ShapeDtypeStruct(kv.shape, jnp.bfloat16)],
        in_specs=[VMEM] * (4 + CHIPS),
        out_specs=[VMEM] * 4,
        scratch_shapes=[pltpu.VMEM((2 * side, PAIR), jnp.bfloat16)] * 4
        + [pltpu.VMEM((2, 2 * side), jnp.float32)] * 2
        + [pltpu.VMEM((2 * side, WIDTH), jnp.float32)] * 2,
        compiler_params=pltpu.CompilerParams(vmem_limit_bytes=40 * 1024 * 1024),
        name="attend",
    )(kv, kcol, qrow, slice_o, *parts)


def unpack_q(chunk, slice_dq, parts):
    rows = parts[1].shape[1]
    kept = rows - slice_dq.shape[0]

    def kernel(chunk_ref, slice_ref, *rest):
        out = rest[-1]
        cols = [pl.ds(pl.multiple_of(chunk_ref[r] * PAIR, PAIR), PAIR) for r in range(N_INNER)]
        out[pl.ds(0, kept), cols[0]] = rest[0][pl.ds(0, kept), :].astype(jnp.float32)
        out[pl.ds(kept, rows - kept), cols[0]] = slice_ref[...].astype(jnp.float32)
        out[:, cols[1]] = rest[0][pl.ds(kept, rows), :].astype(jnp.float32)
        for r in range(2, N_INNER):
            out[:, cols[r]] = rest[r // 2][r % 2].astype(jnp.float32)

    return pl.pallas_call(
        kernel,
        out_shape=jax.ShapeDtypeStruct((rows, N_INNER * PAIR), jnp.float32),
        in_specs=[SMEM] + [VMEM] * (1 + CHIPS),
        out_specs=VMEM,
        name="unpack_q",
    )(chunk, slice_dq, *parts)


def unpack_kv(dkv):
    rows = dkv.shape[1] // 2

    def kernel(in_ref, dk_ref, dv_ref):
        for j in range(N_INNER):
            cols = pl.ds(j * PAIR, PAIR)
            dk_ref[:, cols] = in_ref[j, pl.ds(0, rows), :].astype(jnp.float32)
            dv_ref[:, cols] = in_ref[j, pl.ds(rows, rows), :].astype(jnp.float32)

    return pl.pallas_call(
        kernel,
        out_shape=[jax.ShapeDtypeStruct((rows, N_INNER * PAIR), jnp.float32)] * 2,
        in_specs=[VMEM],
        out_specs=[VMEM] * 2,
        name="unpack_kv",
    )(dkv)


def shards(queries, keys, values, grad_out, lse, delta, span_table):
    outer_count = lax.axis_size("outer")
    outer_idx = lax.axis_index("outer")
    inner_idx = lax.axis_index("inner")
    rows = queries.shape[0]
    half = rows // 2
    to_wrap = (outer_idx == 0).astype(jnp.int32)
    from_wrap = (outer_idx == outer_count - 1).astype(jnp.int32)
    chunk = jnp.stack([moved_inner(inner_idx, dz - to_wrap, dc) for dz in TURNS for dc in range(2)])
    senders = jnp.stack([moved_inner(inner_idx, from_wrap - dz, dc) for dz in TURNS for dc in range(2)])

    axes = ("outer", "inner")
    first_leg, second_leg = long_way(outer_count, False)

    kv = lax.all_to_all(pack_kv(keys, values), "inner", 0, 0, tiled=True)

    slice_o = lax.dynamic_slice_in_dim(grad_out, chunk[0] * PAIR, PAIR, 1)
    middle = lax.ppermute(slice_o, axes, first_leg)
    slice_o = jnp.where(outer_idx % PLANE == 0, middle, slice_o)

    stats = jnp.stack([lse.T.reshape(N_INNER, PAIR), delta.T.reshape(N_INNER, PAIR)], axis=1)
    own_stats = jnp.pad(stats, ((0, 0), (0, STAT_ROWS - 2), (0, 0)))
    stats = jnp.pad(stats, ((0, 0), (2, STAT_ROWS - 4), (0, 0)))
    crossed = to_sibling(pack_for_sibling(chunk, queries, grad_out, stats))
    sent = pack_q(chunk, queries, grad_out, own_stats, crossed)
    slice_o = lax.ppermute(slice_o, axes, send_pairs(outer_count, TURNS[0], False, crossing=False) + second_leg)
    parts = [lax.ppermute(x, axes, send_pairs(outer_count, dz, False)) for dz, x in zip(TURNS, sent)]

    first = span_table[:, 0].reshape(outer_count, N_INNER)
    key_c = lax.dynamic_index_in_dim(first, outer_idx, 0, keepdims=False)
    query_c = lax.dynamic_index_in_dim(first, (outer_idx + 1) % outer_count, 0, keepdims=False)[senders]
    kcol = jnp.repeat(key_c, half)[:, None]
    qrow = jnp.repeat(query_c, half)[None, :]

    own_dq, sibling_dq, slice_dq, dkv = attend(kv, parts, slice_o, kcol, qrow)
    dkv = lax.all_to_all(dkv, "inner", 0, 0, tiled=True)
    first_leg, second_leg = long_way(outer_count, True)
    middle = lax.ppermute(slice_dq, axes, first_leg)
    sent = pack_dq(own_dq, to_sibling(sibling_dq))
    back = [lax.ppermute(x, axes, send_pairs(outer_count, dz, True)) for dz, x in zip(TURNS, sent)]
    slice_dq = jnp.where(outer_idx % PLANE == PLANE - 1, middle, slice_dq)
    slice_dq = lax.ppermute(slice_dq, axes, send_pairs(outer_count, TURNS[0], True, crossing=False) + second_leg)
    grad_k, grad_v = unpack_kv(dkv)
    back, grad_k, grad_v = lax.optimization_barrier((back, grad_k, grad_v))
    grad_q = unpack_q(chunk, slice_dq, back)
    return grad_q, grad_k, grad_v


def solution(mesh):
    placed = P(("outer", "inner"), None)
    return jax.shard_map(
        shards,
        mesh=mesh,
        in_specs=(placed,) * 6 + (P(),),
        out_specs=(placed,) * 3,
        check_vma=False,
    )
```
